32 devices in a mesh: group: 2 (over y), head: 4 (over z), row: 2 (over x), sub: 2 (over core).
Axes of the slice: x: 2, y: 2, z: 4, core: 2. Of those that a mesh axis runs over, the one named last changes fastest.
Arguments:
- query_latent: bfloat16 [256, 1536], P(('group', 'row')), parts along dimension 0, may hold values from -6 to 6
- kv_cache: bfloat16 [256, 128, 512], P(('group', 'row', 'head')), parts along dimension 0, may hold values from -70 to 70
- row_lengths: int32 [256], P(('group', 'row')), parts along dimension 0, may hold values from 1 to 128
- head_map: int32 [128], replicated, may hold values from 0 to 127, as said below
- uq_stored: bfloat16 [128, 1536, 128], P('sub', 'head', 'row'), may hold values from -0.15625 to 0.15625
- uk_stored: bfloat16 [128, 512, 128], P('sub', 'head', 'row'), may hold values from -0.25 to 0.25
- uv_stored: bfloat16 [128, 512, 128], P('sub', 'head', 'row'), may hold values from -0.25 to 0.25
- out_stored: bfloat16 [128, 128, 7168], P('sub', 'head', 'row'), may hold values from -0.5 to 0.5
Outputs:
- attn_output: bfloat16 [256, 7168], P(('group', 'head', 'sub'), 'row'), parts along dimension 0
The draws below stay inside these ranges and needn't reach their ends.
There are 2 independent parts, one for each index of `group`. The reference program is written for one: setup_inputs(seed, part) draws one part's arguments, and reference() takes and returns one part's arrays. A program takes and returns all parts, laid end to end along the dimension named above; an argument that names none is the same for every part. Nothing has to cross between parts.
Inputs may be any that keep to these rules, and one draw needn't show every extreme that they name: `head_map`: slots s * 64 to (s + 1) * 64 - 1 hold every head of that same range once.
All inputs are finite; a program needn't handle non-finite values.
Results may differ from the reference program's by a relative error of at most 0.012.
Values may be sent and summed in bfloat16 or wider, within the bound.
A program may use at most 128 MiB of HBM per device.

```python
import math
import jax
import jax.numpy as jnp
from jax import lax

H = 128
QL = 1536
KL = 512
DH = 128
D = 7168
ROWS_DEV = 64
MAXLEN = 128
BATCH = 128
SLOTS = 64


def draw_kv_cache(key, part):
    key = jax.random.fold_in(key, 11)
    first_key = jax.random.fold_in(key, 1)
    base = jnp.clip(jax.random.normal(first_key, (BATCH, MAXLEN, KL), jnp.float32), -6.0, 6.0)
    return base.astype(jnp.bfloat16)


def draw_row_lengths(key, part):
    key = jax.random.fold_in(key, 5)
    blocks = BATCH // ROWS_DEV
    rows_all = jnp.arange(BATCH, dtype=jnp.int32)
    block_of = rows_all // ROWS_DEV
    ceiling = jnp.maximum(MAXLEN * (block_of + 1) // blocks, 1)
    drawn = 1 + jax.random.randint(key, (BATCH,), 0, ceiling)
    return jnp.where(rows_all == BATCH - 1, MAXLEN, drawn).astype(jnp.int32)


def draw_head_map(key, part):
    key = jax.random.fold_in(key, 7)
    halves = []
    for index in range(H // SLOTS):
        shuffled = jax.random.permutation(jax.random.fold_in(key, index), SLOTS)
        halves.append(shuffled.astype(jnp.int32) + index * SLOTS)
    return jnp.concatenate(halves).astype(jnp.int32)


def level_of(key, shape, split, least, top_value):
    gain = 1.0
    for axis_at, blocks in split:
        heights = jax.random.uniform(jax.random.fold_in(jax.random.fold_in(key, 6), axis_at), (blocks,), jnp.float32, least / len(split), top_value / len(split))
        gain = gain * jnp.repeat(jnp.exp(heights), shape[axis_at] // blocks).reshape((-1,) + (1,) * (len(shape) - 1 - axis_at))
    return gain


def centred(rng, extent, spread, limit, cuts=(), kind=jnp.bfloat16):
    entries = jax.random.normal(rng, extent, jnp.float32) * spread
    if len(cuts) > 0:
        entries = level_of(rng, extent, cuts, -0.22, 0.18) * entries
    return jnp.clip(entries, min=-limit, max=limit).astype(kind)


def setup_inputs(seed: int = 0, part: int = 0) -> dict:
    key_list = jax.random.split(jax.random.key(seed), 9)
    own_keys = jax.random.split(jax.random.fold_in(key_list[8], part), 9)
    query_latent = centred(own_keys[0], (BATCH, QL), 1.0, 6.0, ((0, 2),))
    kv_cache = draw_kv_cache(jax.random.fold_in(jax.random.fold_in(key_list[8], part), 71), part)
    row_lengths = draw_row_lengths(jax.random.fold_in(jax.random.fold_in(key_list[8], part), 71), part)
    head_map = draw_head_map(jax.random.fold_in(key_list[8], 71), part)
    uq_stored = centred(key_list[4], (H, QL, DH), QL ** -0.5, 0.15625, ((0, 2), (1, 4), (2, 2)))
    uk_stored = centred(key_list[5], (H, KL, DH), KL ** -0.5, 0.25, ((0, 2), (1, 4), (2, 2)))
    uv_stored = centred(key_list[6], (H, KL, DH), KL ** -0.5, 0.25, ((0, 2), (1, 4), (2, 2)))
    out_stored = centred(key_list[7], (H, DH, D), DH ** -0.5, 0.5, ((0, 2), (1, 4), (2, 2)))
    return dict(query_latent=query_latent, kv_cache=kv_cache, row_lengths=row_lengths, head_map=head_map, uq_stored=uq_stored, uk_stored=uk_stored, uv_stored=uv_stored, out_stored=out_stored)


def reference(query_latent, kv_cache, row_lengths, head_map, uq_stored, uk_stored, uv_stored, out_stored):
    slot_order = jnp.argsort(head_map).astype(jnp.int32)
    query_up = jnp.take(uq_stored, slot_order, axis=0)
    key_up = jnp.take(uk_stored, slot_order, axis=0)
    value_up = jnp.take(uv_stored, slot_order, axis=0)
    score_scale = 1.0 / math.sqrt(DH)
    positions = jnp.arange(MAXLEN, dtype=jnp.int32)
    alive = positions[None, :] < row_lengths[:, None]
    cache_wide = kv_cache.astype(jnp.float32)

    def per_head(summed, stacked):
        query_w, key_w, value_w, out_w = stacked
        absorbed_q = jnp.dot(query_w, key_w.T, preferred_element_type=jnp.float32).astype(jnp.bfloat16)
        absorbed_o = jnp.dot(value_w, out_w, preferred_element_type=jnp.float32).astype(jnp.bfloat16)
        query_lat = jnp.dot(query_latent, absorbed_q, preferred_element_type=jnp.float32).astype(jnp.bfloat16)
        scores = jnp.einsum('bk,btk->bt', query_lat.astype(jnp.float32), cache_wide, precision=lax.Precision.HIGHEST) * score_scale
        scores = jnp.where(alive, scores, -1e+30)
        highest = lax.optimization_barrier(jnp.max(scores, axis=1, keepdims=True))
        weights = jnp.where(alive, jnp.exp(scores - highest), 0.0)
        probs = weights / lax.optimization_barrier(jnp.sum(weights, axis=1, keepdims=True))
        attended = jnp.einsum('bt,btk->bk', probs, cache_wide, precision=lax.Precision.HIGHEST).astype(jnp.bfloat16)
        return (summed + jnp.dot(attended, absorbed_o, preferred_element_type=jnp.float32), None)
    start_sum = jnp.zeros((BATCH, D), jnp.float32)
    summed, _ = lax.scan(per_head, start_sum, (query_up, key_up, value_up, out_stored))
    return summed.astype(jnp.bfloat16)
```

```python
import functools
import math

import jax
import jax.numpy as jnp
from jax import lax
from jax.experimental import pallas as pl
from jax.experimental.pallas import tpu as pltpu
from jax.sharding import PartitionSpec as P

DH = 128


def form_pair(query_up, key_up, value_up, out_up):
    absorbed_q = jnp.einsum(
        "hqd,hkd->hqk", query_up, key_up, preferred_element_type=jnp.float32
    ).astype(jnp.bfloat16)
    absorbed_o = jnp.einsum(
        "hkd,hdo->hko", value_up, out_up, preferred_element_type=jnp.float32
    ).astype(jnp.bfloat16)
    return (absorbed_q, absorbed_o)


def attend(running, queries, lengths, block_rows, first_pos, score_scale):
    best, mass, accum = running
    width = block_rows.shape[1]
    scores = (
        jnp.einsum("rhk,rtk->rht", queries, block_rows, preferred_element_type=jnp.float32)
        * score_scale
    )
    positions = first_pos + jnp.arange(width, dtype=jnp.int32)
    alive = (positions[None, :] < lengths[:, None])[:, None, :]
    scores = jnp.where(alive, scores, -1e30)
    newest = jnp.maximum(best, jnp.max(scores, axis=2))
    weights = jnp.where(alive, jnp.exp(scores - newest[:, :, None]), 0.0)
    factor = jnp.exp(best - newest)
    mass = mass * factor + jnp.sum(weights, axis=2)
    accum = accum * factor[:, :, None] + jnp.einsum(
        "rht,rtk->rhk", weights, block_rows.astype(jnp.float32), precision=lax.Precision.HIGHEST
    )
    return (newest, mass, accum)


def local_general(
    query_latent, kv_cache, row_lengths, head_map, uq_stored, uk_stored, uv_stored, out_stored
):
    slots = uq_stored.shape[0]
    first_slot = lax.axis_index("sub") * slots
    local_map = lax.dynamic_slice_in_dim(head_map, first_slot, slots, 0)
    slot_order = jnp.argsort(local_map)
    query_up = jnp.take(uq_stored, slot_order, axis=0)
    key_up = jnp.take(uk_stored, slot_order, axis=0)
    value_up = jnp.take(uv_stored, slot_order, axis=0)
    query_up, key_up, value_up, out_up = (
        lax.all_to_all(query_up, "head", split_axis=0, concat_axis=1, tiled=True),
        lax.all_to_all(key_up, "head", split_axis=0, concat_axis=1, tiled=True),
        lax.all_to_all(value_up, "head", split_axis=0, concat_axis=1, tiled=True),
        lax.all_to_all(out_stored, "head", split_axis=0, concat_axis=1, tiled=True),
    )
    query_up, key_up, value_up = (
        lax.all_gather(query_up, "row", axis=2, tiled=True),
        lax.all_gather(key_up, "row", axis=2, tiled=True),
        lax.all_gather(value_up, "row", axis=2, tiled=True),
    )
    absorbed_q, absorbed_o = form_pair(query_up, key_up, value_up, out_up)
    query_lat = jnp.einsum(
        "rq,hqk->rhk", query_latent, absorbed_q, preferred_element_type=jnp.float32
    ).astype(jnp.bfloat16)
    score_scale = 1.0 / math.sqrt(DH)
    head_count = query_lat.shape[1]
    latent_width = query_lat.shape[2]
    piece = lax.all_gather(kv_cache, "head", axis=0, tiled=True)
    count = piece.shape[0]
    half = piece.shape[1] // 2
    state = (
        jnp.full((count, head_count), -1e30, jnp.float32),
        jnp.zeros((count, head_count), jnp.float32),
        jnp.zeros((count, head_count, latent_width), jnp.float32),
    )
    state = attend(state, query_lat, row_lengths, piece[:, :half], 0, score_scale)
    state = attend(state, query_lat, row_lengths, piece[:, half:], half, score_scale)
    best, mass, accum = state
    result = accum / mass[:, :, None]
    attended = result.astype(jnp.bfloat16)
    gathered = lax.all_gather(attended, "row", axis=0, tiled=True)
    summed = lax.psum_scatter(
        jnp.einsum("rhk,hko->ro", gathered, absorbed_o, preferred_element_type=jnp.float32),
        ("head", "sub"),
        scatter_dimension=0,
        tiled=True,
    )
    return summed.astype(jnp.bfloat16)


MESH = pl.DeviceIdType.MESH
F32 = jnp.float32
BF16 = jnp.bfloat16


def attention_kernel(
    n_row,
    n_head,
    scale,
    ql_ref,
    kv_ref,
    mask_ref,
    uq_ref,
    uk_ref,
    uv_ref,
    v_out,
    lat,
    q_send,
    q_recv,
    uk_send,
    uk_recv,
    uv_send,
    uv_recv,
    wide,
    x_send,
    x_recv,
    y_send,
    y_recv,
    v_send,
    send_sem,
    recv_sem,
    own_sem,
):
    n = n_row * n_head
    row = lax.axis_index("row")
    head = lax.axis_index("head")
    me = row * n_head + head
    slots, part, half = uq_ref.shape
    per = slots // n
    pairs = per // 2
    rows = ql_ref.shape[0]
    batch = rows * n_row
    own = batch // n
    peers = [lax.rem(me + k, n) for k in range(1, n)]

    def place(peer):
        return {"row": peer // n_head, "head": lax.rem(peer, n_head)}

    def remote(phase, k, src, dst, peer):
        return pltpu.make_async_remote_copy(
            src_ref=src,
            dst_ref=dst,
            send_sem=send_sem.at[phase, k],
            recv_sem=recv_sem.at[phase, me],
            device_id=place(peer),
            device_id_type=MESH,
        )

    def arrival(phase, src, dst):
        for k in range(1, n):
            peer = lax.rem(me + k, n)
            pltpu.make_async_remote_copy(
                src_ref=src.at[peer],
                dst_ref=dst.at[peer],
                send_sem=send_sem.at[phase, k],
                recv_sem=recv_sem.at[phase, peer],
                device_id=place(peer),
                device_id_type=MESH,
            ).wait_recv()

    def spread(phase, src, dst):
        copies = []
        for k in range(1, n):
            peer = lax.rem(me + k, n)
            copy = remote(phase, k, src.at[peer], dst.at[me], peer)
            copy.start()
            copies.append(copy)
        return copies

    barrier = pltpu.get_barrier_semaphore()
    for peer in peers:
        pl.semaphore_signal(barrier, inc=1, device_id=place(peer), device_id_type=MESH)
    pl.semaphore_wait(barrier, n - 1)

    columns = pl.ds(pl.multiple_of(head * part, 128), part)
    pending = []
    for k in range(1, n_row):
        other = lax.rem(row + k, n_row)
        copy = remote(0, k, ql_ref.at[:, columns], lat.at[row], other * n_head + head)
        copy.start()
        pending.append(copy)
    lat[row] = ql_ref[:, columns]

    def pack(pair, carry):
        peer = pair // pairs
        at = lax.rem(pair, pairs)
        uk_send[peer, at] = jnp.concatenate([uk_ref[2 * pair], uk_ref[2 * pair + 1]], axis=1)
        uv_send[peer, at] = jnp.concatenate([uv_ref[2 * pair], uv_ref[2 * pair + 1]], axis=1)
        return carry

    lax.fori_loop(0, slots // 2, pack, 0)

    for k in range(1, n_row):
        other = lax.rem(row + k, n_row)
        pltpu.make_async_remote_copy(
            src_ref=lat.at[other],
            dst_ref=lat.at[other],
            send_sem=send_sem.at[0, k],
            recv_sem=recv_sem.at[0, other * n_head + head],
            device_id=place(other * n_head + head),
            device_id_type=MESH,
        ).wait_recv()
    latent = lat[...].reshape(batch, part)

    for k in range(1, n + 1):
        peer = lax.rem(me + k, n)
        for at in range(pairs):
            slot = peer * per + 2 * at
            first = jnp.dot(latent, uq_ref[slot], preferred_element_type=F32)
            second = jnp.dot(latent, uq_ref[slot + 1], preferred_element_type=F32)
            both = jnp.concatenate([first, second], axis=1).astype(BF16)
            if k < n:
                q_send[peer, at] = both
            else:
                q_recv[me, at] = both
        if k < n:
            copy = remote(1, k, q_send.at[peer], q_recv.at[me], peer)
            copy.start()
            pending.append(copy)
    pending += spread(2, uk_send, uk_recv)
    uk_recv[me] = uk_send[me]
    uv_recv[me] = uv_send[me]

    arrival(1, q_send, q_recv)
    arrival(2, uk_send, uk_recv)

    def joined(ref, at, which):
        blocks = []
        for r in range(n_row):
            block = ref[r * n_head : (r + 1) * n_head, at]
            block = block.reshape(-1, block.shape[-1])
            blocks.append(block[:, which * half : (which + 1) * half])
        return jnp.concatenate(blocks, axis=1)

    for at in range(pairs):
        sums = []
        for r in range(n_row):
            total = q_recv[r * n_head, at].astype(F32)
            for h in range(1, n_head):
                total = total + q_recv[r * n_head + h, at].astype(F32)
            sums.append(total.astype(BF16))
        for which in range(2):
            query = jnp.concatenate([s[:, which * half : (which + 1) * half] for s in sums], axis=1)
            key_up = joined(uk_recv, at, which)
            wide[:, 2 * at + which, :] = lax.dot_general(
                query, key_up, (((1,), (1,)), ((), ())), preferred_element_type=F32
            )
    for k in range(1, n + 1):
        peer = lax.rem(me + k, n)
        block = wide[pl.ds(peer * own, own)].reshape(own * per, -1).astype(BF16)
        if k < n:
            x_send[peer] = block
            copy = remote(3, k, x_send.at[peer], x_recv.at[me], peer)
            copy.start()
            pending.append(copy)
        else:
            x_recv[me] = block
    pending += spread(4, uv_send, uv_recv)
    arrival(3, x_send, x_recv)

    for b in range(own):
        query = jnp.concatenate(
            [x_recv[p].astype(F32)[b * per : (b + 1) * per] for p in range(n)], axis=0
        ).astype(BF16)
        cache = kv_ref[b]
        scores = (
            lax.dot_general(query, cache, (((1,), (1,)), ((), ())), preferred_element_type=F32)
            * scale
        )
        alive = mask_ref[b : b + 1, :] > 0
        scores = jnp.where(alive, scores, -1e30)
        top = jnp.max(scores, axis=1, keepdims=True)
        weights = jnp.where(alive, jnp.exp(scores - top), 0.0)
        mass = jnp.sum(weights, axis=1, keepdims=True)
        mixed = jnp.dot(weights.astype(BF16), cache, preferred_element_type=F32) / mass
        for p in range(n):
            wide[p * own + b] = mixed[p * per : (p + 1) * per]
    for k in range(1, n + 1):
        peer = lax.rem(me + k, n)
        block = wide[pl.ds(peer * own, own)].reshape(own * per, -1).astype(BF16)
        if k < n:
            y_send[peer] = block
            copy = remote(5, k, y_send.at[peer], y_recv.at[me], peer)
            copy.start()
            pending.append(copy)
        else:
            y_recv[me] = block
    arrival(4, uv_send, uv_recv)
    arrival(5, y_send, y_recv)

    wide[...] = y_recv[...].astype(F32).reshape(wide.shape)
    values = []
    for at in range(pairs):
        for which in range(2):
            mixed = wide[:, 2 * at + which, :].astype(BF16)
            values.append(
                jnp.dot(mixed, joined(uv_recv, at, which), preferred_element_type=F32).astype(BF16)
            )
    share = values[0].shape[1] // n_head
    for h in range(n_head):
        v_send[h] = jnp.concatenate([v[:, h * share : (h + 1) * share] for v in values], axis=1)
    for k in range(1, n):
        peer = lax.rem(me + k, n)
        copy = remote(6, k, v_send.at[lax.rem(peer, n_head)], v_out.at[me], peer)
        copy.start()
        pending.append(copy)
    v_out[me] = v_send[head]
    arrival(6, v_out, v_out)
    for copy in pending:
        copy.wait_send()


def sum_kernel(n_head, n_sub, part_ref, out_ref, recv, send_sem, recv_sem):
    n = n_head * n_sub
    me = lax.axis_index("head") * n_sub + lax.axis_index("sub")
    own = out_ref.shape[0]

    def place(peer):
        return {"head": peer // n_sub, "sub": lax.rem(peer, n_sub)}

    barrier = pltpu.get_barrier_semaphore()
    for k in range(1, n):
        pl.semaphore_signal(
            barrier, inc=1, device_id=place(lax.rem(me + k, n)), device_id_type=MESH
        )
    pl.semaphore_wait(barrier, n - 1)
    copies = []
    for k in range(1, n):
        peer = lax.rem(me + k, n)
        copy = pltpu.make_async_remote_copy(
            src_ref=part_ref.at[peer],
            dst_ref=recv.at[me],
            send_sem=send_sem.at[k],
            recv_sem=recv_sem.at[me],
            device_id=place(peer),
            device_id_type=MESH,
        )
        copy.start()
        copies.append(copy)
    total = part_ref[me].astype(F32)
    for k in range(1, n):
        peer = lax.rem(me + k, n)
        pltpu.make_async_remote_copy(
            src_ref=part_ref.at[peer],
            dst_ref=recv.at[peer],
            send_sem=send_sem.at[k],
            recv_sem=recv_sem.at[peer],
            device_id=place(peer),
            device_id_type=MESH,
        ).wait_recv()
        total = total + recv[peer].astype(F32)
    out_ref[...] = total.astype(out_ref.dtype)
    for copy in copies:
        copy.wait_send()


def local_fast(
    n_row,
    n_head,
    n_sub,
    query_latent,
    kv_cache,
    row_lengths,
    head_map,
    uq_stored,
    uk_stored,
    uv_stored,
    out_stored,
):
    n = n_row * n_head
    slots, part, half = uq_stored.shape
    own, width, latent = kv_cache.shape
    rows = query_latent.shape[0]
    batch = rows * n_row
    per = slots // n
    k_part = uk_stored.shape[1]
    depth = half * n_row
    share = depth // n_head
    lengths = lax.dynamic_slice_in_dim(row_lengths, lax.axis_index("head") * own, own, 0)
    mask = (jnp.arange(width, dtype=jnp.int32)[None, :] < lengths[:, None]).astype(jnp.int32)
    vmem = pl.BlockSpec(memory_space=pltpu.VMEM)
    values = pl.pallas_call(
        functools.partial(attention_kernel, n_row, n_head, 1.0 / math.sqrt(DH)),
        out_shape=jax.ShapeDtypeStruct((n, batch, per * share), BF16),
        in_specs=[vmem] * 6,
        out_specs=vmem,
        scratch_shapes=[
            pltpu.VMEM((n_row, rows, part), BF16),
            pltpu.VMEM((n, per // 2, batch, 2 * half), BF16),
            pltpu.VMEM((n, per // 2, batch, 2 * half), BF16),
            pltpu.VMEM((n, per // 2, k_part, 2 * half), BF16),
            pltpu.VMEM((n, per // 2, k_part, 2 * half), BF16),
            pltpu.VMEM((n, per // 2, k_part, 2 * half), BF16),
            pltpu.VMEM((n, per // 2, k_part, 2 * half), BF16),
            pltpu.VMEM((batch, per, latent), F32),
            pltpu.VMEM((n, own * per, latent), BF16),
            pltpu.VMEM((n, own * per, latent), BF16),
            pltpu.VMEM((n, own * per, latent), BF16),
            pltpu.VMEM((n, own * per, latent), BF16),
            pltpu.VMEM((n_head, batch, per * share), BF16),
            pltpu.SemaphoreType.DMA((7, n)),
            pltpu.SemaphoreType.DMA((7, n)),
            pltpu.SemaphoreType.DMA,
        ],
        compiler_params=pltpu.CompilerParams(
            collective_id=0, has_side_effects=True, vmem_limit_bytes=56 * 1024 * 1024
        ),
    )(query_latent, kv_cache, mask, uq_stored, uk_stored, uv_stored)
    first_slot = lax.axis_index("sub") * slots
    local_map = lax.dynamic_slice_in_dim(head_map, first_slot, slots, 0)
    slot_order = jnp.argsort(local_map)
    values = values.reshape(n, batch, per, share).transpose(0, 2, 1, 3)
    values = jnp.take(values.reshape(slots, batch, share), slot_order, axis=0)
    values = values.transpose(1, 0, 2).reshape(batch, slots * share)
    partial = jnp.dot(
        values, out_stored.reshape(slots * share, -1), preferred_element_type=F32
    ).astype(BF16)
    peers = n_head * n_sub
    partial = partial.reshape(peers, batch // peers, -1)
    return pl.pallas_call(
        functools.partial(sum_kernel, n_head, n_sub),
        out_shape=jax.ShapeDtypeStruct(partial.shape[1:], BF16),
        in_specs=[vmem],
        out_specs=vmem,
        scratch_shapes=[
            pltpu.VMEM(partial.shape, BF16),
            pltpu.SemaphoreType.DMA((peers,)),
            pltpu.SemaphoreType.DMA((peers,)),
        ],
        compiler_params=pltpu.CompilerParams(
            collective_id=1, has_side_effects=True, vmem_limit_bytes=32 * 1024 * 1024
        ),
    )(partial)


def choose_local(mesh):
    n_row, n_head, n_sub = mesh.shape["row"], mesh.shape["head"], mesh.shape["sub"]

    def local(query_latent, kv_cache, row_lengths, head_map, uq, uk, uv, out_stored):
        args = (query_latent, kv_cache, row_lengths, head_map, uq, uk, uv, out_stored)
        n = n_row * n_head
        batch = query_latent.shape[0] * n_row
        fits = (
            uq.shape[0] % (8 * n) == 0
            and uq.shape[1] % 128 == 0
            and uk.shape[1] % 128 == 0
            and uq.shape[2] % 64 == 0
            and batch % (16 * n) == 0
            and batch % (16 * n_head * n_sub) == 0
        )
        if fits:
            return local_fast(n_row, n_head, n_sub, *args)
        return local_general(*args)

    return local


def solution(mesh):
    in_specs = (
        P(("group", "row"), None),
        P(("group", "row", "head"), None, None),
        P(("group", "row")),
        P(),
        P("sub", "head", "row"),
        P("sub", "head", "row"),
        P("sub", "head", "row"),
        P("sub", "head", "row"),
    )
    out_specs = P(("group", "head", "sub"), "row")
    local = choose_local(mesh)
    return jax.shard_map(local, mesh=mesh, in_specs=in_specs, out_specs=out_specs, check_vma=False)
```

```python
import functools
import math

import jax
import jax.numpy as jnp
from jax import lax
from jax.experimental import pallas as pl
from jax.experimental.pallas import tpu as pltpu
from jax.sharding import PartitionSpec as P

DH = 128


def form_pair(query_up, key_up, value_up, out_up):
    absorbed_q = jnp.einsum(
        "hqd,hkd->hqk", query_up, key_up, preferred_element_type=jnp.float32
    ).astype(jnp.bfloat16)
    absorbed_o = jnp.einsum(
        "hkd,hdo->hko", value_up, out_up, preferred_element_type=jnp.float32
    ).astype(jnp.bfloat16)
    return (absorbed_q, absorbed_o)


def attend(running, queries, lengths, block_rows, first_pos, score_scale):
    best, mass, accum = running
    width = block_rows.shape[1]
    scores = (
        jnp.einsum("rhk,rtk->rht", queries, block_rows, preferred_element_type=jnp.float32)
        * score_scale
    )
    positions = first_pos + jnp.arange(width, dtype=jnp.int32)
    alive = (positions[None, :] < lengths[:, None])[:, None, :]
    scores = jnp.where(alive, scores, -1e30)
    newest = jnp.maximum(best, jnp.max(scores, axis=2))
    weights = jnp.where(alive, jnp.exp(scores - newest[:, :, None]), 0.0)
    factor = jnp.exp(best - newest)
    mass = mass * factor + jnp.sum(weights, axis=2)
    accum = accum * factor[:, :, None] + jnp.einsum(
        "rht,rtk->rhk", weights, block_rows.astype(jnp.float32), precision=lax.Precision.HIGHEST
    )
    return (newest, mass, accum)


def local_general(
    query_latent, kv_cache, row_lengths, head_map, uq_stored, uk_stored, uv_stored, out_stored
):
    slots = uq_stored.shape[0]
    first_slot = lax.axis_index("sub") * slots
    local_map = lax.dynamic_slice_in_dim(head_map, first_slot, slots, 0)
    slot_order = jnp.argsort(local_map)
    query_up = jnp.take(uq_stored, slot_order, axis=0)
    key_up = jnp.take(uk_stored, slot_order, axis=0)
    value_up = jnp.take(uv_stored, slot_order, axis=0)
    query_up, key_up, value_up, out_up = (
        lax.all_to_all(query_up, "head", split_axis=0, concat_axis=1, tiled=True),
        lax.all_to_all(key_up, "head", split_axis=0, concat_axis=1, tiled=True),
        lax.all_to_all(value_up, "head", split_axis=0, concat_axis=1, tiled=True),
        lax.all_to_all(out_stored, "head", split_axis=0, concat_axis=1, tiled=True),
    )
    query_up, key_up, value_up = (
        lax.all_gather(query_up, "row", axis=2, tiled=True),
        lax.all_gather(key_up, "row", axis=2, tiled=True),
        lax.all_gather(value_up, "row", axis=2, tiled=True),
    )
    absorbed_q, absorbed_o = form_pair(query_up, key_up, value_up, out_up)
    query_lat = jnp.einsum(
        "rq,hqk->rhk", query_latent, absorbed_q, preferred_element_type=jnp.float32
    ).astype(jnp.bfloat16)
    score_scale = 1.0 / math.sqrt(DH)
    head_count = query_lat.shape[1]
    latent_width = query_lat.shape[2]
    piece = lax.all_gather(kv_cache, "head", axis=0, tiled=True)
    count = piece.shape[0]
    half = piece.shape[1] // 2
    state = (
        jnp.full((count, head_count), -1e30, jnp.float32),
        jnp.zeros((count, head_count), jnp.float32),
        jnp.zeros((count, head_count, latent_width), jnp.float32),
    )
    state = attend(state, query_lat, row_lengths, piece[:, :half], 0, score_scale)
    state = attend(state, query_lat, row_lengths, piece[:, half:], half, score_scale)
    best, mass, accum = state
    result = accum / mass[:, :, None]
    attended = result.astype(jnp.bfloat16)
    gathered = lax.all_gather(attended, "row", axis=0, tiled=True)
    summed = lax.psum_scatter(
        jnp.einsum("rhk,hko->ro", gathered, absorbed_o, preferred_element_type=jnp.float32),
        ("head", "sub"),
        scatter_dimension=0,
        tiled=True,
    )
    return summed.astype(jnp.bfloat16)


MESH = pl.DeviceIdType.MESH
F32 = jnp.float32
BF16 = jnp.bfloat16


def attention_kernel(
    n_row,
    n_head,
    scale,
    ql_ref,
    kv_ref,
    mask_ref,
    map_ref,
    uq_ref,
    uk_ref,
    uv_ref,
    out_hbm,
    result,
    lat,
    q_send,
    q_recv,
    uk_recv,
    uv_recv,
    wide,
    x_send,
    x_recv,
    y_send,
    y_recv,
    v_send,
    v_recv,
    pick,
    picked,
    out_up,
    part_sums,
    near_sums,
    chip_sums,
    far_sums,
    send_sem,
    recv_sem,
    load_sem,
):
    n = n_row * n_head
    group = lax.axis_index("group")
    sub = lax.axis_index("sub")
    row = lax.axis_index("row")
    head = lax.axis_index("head")
    me = row * n_head + head
    slots, half, part = uq_ref.shape
    per = slots // n
    pairs = per // 2
    rows = ql_ref.shape[0]
    batch = rows * n_row
    own = batch // n
    near = own // 2
    kept = pl.ds(group * (per // 2), per // 2)
    turns = [n_head // 2] + [d for d in range(1, n_head) if d != n_head // 2] + [0]
    shifts = [(dr, dh) for dh in turns for dr in range(n_row) if (dr, dh) != (0, 0)]
    peers = [
        lax.rem(row + dr, n_row) * n_head + lax.rem(head + dh, n_head) for dr, dh in shifts
    ]
    pending = []

    def place(peer):
        return {"row": peer // n_head, "head": lax.rem(peer, n_head)}

    def remote(phase, k, src, dst, slot, device):
        return pltpu.make_async_remote_copy(
            src_ref=src,
            dst_ref=dst,
            send_sem=send_sem.at[phase, k],
            recv_sem=recv_sem.at[phase, slot],
            device_id=device,
            device_id_type=MESH,
        )

    def send(phase, k, src, dst, peer):
        copy = remote(phase, k, src, dst, me, place(peer))
        copy.start()
        pending.append(copy)

    def arrived(phase, k, dst, peer):
        remote(phase, k, dst, dst, peer, place(peer)).wait_recv()

    def send_weights(phase, src, dst):
        for k, peer in enumerate(peers):
            first = peer * per + group * (per // 2)
            send(phase, k, src.at[pl.ds(first, per // 2)], dst.at[me, kept], peer)

    def pass_weights(phase, dst):
        for k, peer in enumerate(peers):
            arrived(phase, k, dst.at[peer, kept], peer)
            block = dst.at[peer, kept]
            copy = remote(phase + 1, k, block, block, peer, {"group": 1 - group})
            copy.start()
            pending.append(copy)

    def await_weights(phase, dst):
        other = pl.ds((1 - group) * (per // 2), per // 2)
        for k, peer in enumerate(peers):
            block = dst.at[peer, other]
            remote(phase + 1, k, block, block, peer, {"group": 1 - group}).wait_recv()

    barrier = pltpu.get_barrier_semaphore()
    for peer in peers:
        pl.semaphore_signal(barrier, inc=1, device_id=place(peer), device_id_type=MESH)
    pl.semaphore_signal(barrier, inc=1, device_id={"group": 1 - group}, device_id_type=MESH)
    pl.semaphore_signal(barrier, inc=1, device_id={"sub": 1 - sub}, device_id_type=MESH)
    pl.semaphore_wait(barrier, n + 1)

    columns = pl.ds(pl.multiple_of(head * part, 128), part)
    others = [lax.rem(row + k, n_row) for k in range(1, n_row)]
    for k, other in enumerate(others):
        send(0, k, ql_ref.at[:, columns], lat.at[row], other * n_head + head)
    send_weights(2, uk_ref, uk_recv)
    load = pltpu.make_async_copy(out_hbm, out_up, load_sem)
    load.start()
    lat[row] = ql_ref[:, columns]
    mine = pl.ds(me * per, per)
    uk_recv[me] = uk_ref[mine]
    uv_recv[me] = uv_ref[mine]
    for k, other in enumerate(others):
        arrived(0, k, lat.at[other], other * n_head + head)
    latent = lat[...].reshape(batch, part)

    for k, peer in enumerate(peers + [me]):
        for at in range(pairs):
            two = uq_ref[pl.ds(peer * per + 2 * at, 2)].reshape(2 * half, part)
            both = lax.dot_general(
                latent, two, (((1,), (1,)), ((), ())), preferred_element_type=F32
            ).astype(BF16)
            if k < n - 1:
                q_send[peer, at] = both
            else:
                q_recv[me, at] = both
        if k < n - 1:
            send(1, k, q_send.at[peer], q_recv.at[me], peer)
    send_weights(8, uv_ref, uv_recv)
    pass_weights(2, uk_recv)

    share = out_hbm.shape[1]
    spots = lax.broadcasted_iota(jnp.int32, (share, slots * share), 1)
    spots = spots - lax.broadcasted_iota(jnp.int32, (share, slots * share), 0)

    def mark(slot, carry):
        lanes = spots == map_ref[slot] * share
        first = pl.multiple_of(slot * share, share)
        pick[pl.ds(first, share), :] = jnp.where(lanes, 1.0, 0.0).astype(BF16)
        return carry

    lax.fori_loop(0, slots, mark, 0)

    for k, peer in enumerate(peers):
        arrived(1, k, q_recv.at[peer], peer)
    queries = []
    for at in range(pairs):
        sums = []
        for r in range(n_row):
            total = q_recv[r * n_head, at].astype(F32)
            for h in range(1, n_head):
                total = total + q_recv[r * n_head + h, at].astype(F32)
            sums.append(total.astype(BF16))
        for which in range(2):
            queries.append(
                jnp.concatenate([s[:, which * half : (which + 1) * half] for s in sums], axis=1)
            )
    await_weights(2, uk_recv)

    def joined(ref, slot):
        return jnp.concatenate(
            [
                jnp.concatenate([ref[r * n_head + h, slot] for h in range(n_head)], axis=1)
                for r in range(n_row)
            ],
            axis=0,
        )

    for slot in range(per):
        wide[:, slot, :] = jnp.dot(
            queries[slot], joined(uk_recv, slot), preferred_element_type=F32
        )
    for part_at in range(2):
        for k, peer in enumerate(peers + [me]):
            block = wide[pl.ds(peer * own + part_at * near, near)]
            block = block.reshape(near * per, -1).astype(BF16)
            if k < n - 1:
                x_send[part_at, peer] = block
                send(
                    4 + part_at, k, x_send.at[part_at, peer], x_recv.at[part_at, me], peer
                )
            else:
                x_recv[part_at, me] = block
    pass_weights(8, uv_recv)

    for part_at in range(2):
        for k, peer in enumerate(peers):
            arrived(4 + part_at, k, x_recv.at[part_at, peer], peer)
        wanted = x_recv[part_at].astype(F32)
        scores = []
        for b in range(near):
            query = wanted[:, b * per : (b + 1) * per].reshape(slots, -1).astype(BF16)
            score = (
                lax.dot_general(
                    query,
                    kv_ref[part_at * near + b],
                    (((1,), (1,)), ((), ())),
                    preferred_element_type=F32,
                )
                * scale
            )
            at = part_at * near + b
            scores.append(jnp.where(mask_ref[at : at + 1, :] > 0, score, -1e30))
        stacked = jnp.concatenate(scores, axis=0)
        top = jnp.max(stacked, axis=1, keepdims=True)
        weights = jnp.exp(stacked - top)
        mass = jnp.sum(weights, axis=1, keepdims=True)
        weights = (weights / mass).astype(BF16)
        for b in range(near):
            mixed = jnp.dot(
                weights[b * slots : (b + 1) * slots],
                kv_ref[part_at * near + b],
                preferred_element_type=F32,
            )
            for p in range(n):
                wide[p * own + part_at * near + b] = mixed[p * per : (p + 1) * per]
        for k, peer in enumerate(peers + [me]):
            block = wide[pl.ds(peer * own + part_at * near, near)]
            block = block.reshape(near * per, -1).astype(BF16)
            if k < n - 1:
                y_send[part_at, peer] = block
                send(
                    6 + part_at, k, y_send.at[part_at, peer], y_recv.at[part_at, me], peer
                )
            else:
                y_recv[part_at, me] = block
    await_weights(8, uv_recv)
    for part_at in range(2):
        for k, peer in enumerate(peers):
            arrived(6 + part_at, k, y_recv.at[part_at, peer], peer)
        for p in range(n):
            first = p * own + part_at * near
            wide[first : first + near] = (
                y_recv[part_at, p].astype(F32).reshape(near, per, wide.shape[2])
            )
    values = []
    for slot in range(per):
        values.append(
            lax.dot_general(
                wide[:, slot, :].astype(BF16),
                joined(uv_recv, slot),
                (((1,), (1,)), ((), ())),
                preferred_element_type=F32,
            ).astype(BF16)
        )
    for h in range(n_head):
        v_send[h] = jnp.concatenate([v[:, h * share : (h + 1) * share] for v in values], axis=1)
    heads = [lax.rem(head + d, n_head) for d in turns]
    v_recv[me] = v_send[head]
    for k, other in enumerate(heads[:-1]):
        send(10, k, v_send.at[other], v_recv.at[me], row * n_head + other)

    def forward(k, peer):
        for i, other in enumerate(others):
            copy = remote(
                11,
                k * (n_row - 1) + i,
                v_recv.at[peer],
                v_recv.at[peer],
                peer,
                place(other * n_head + head),
            )
            copy.start()
            pending.append(copy)

    deep = per * share

    def spread(peer, fresh):
        rows_of = pl.ds(pl.multiple_of(peer * deep, deep), deep)
        term = jnp.dot(v_recv[peer], pick[rows_of, :], preferred_element_type=F32)
        picked[...] = term if fresh else picked[...] + term

    forward(n_head - 1, me)
    spread(me, True)
    for k, other in enumerate(heads[:-1]):
        peer = row * n_head + other
        arrived(10, k, v_recv.at[peer], peer)
        forward(k, peer)
        spread(peer, False)
    for i, away in enumerate(others):
        for k, other in enumerate([heads[-1]] + heads[:-1]):
            peer = away * n_head + other
            remote(
                11, 0, v_recv.at[peer], v_recv.at[peer], peer, place(away * n_head + head)
            ).wait_recv()
            spread(peer, False)

    load.wait()
    chunks, step = part_sums.shape[0], part_sums.shape[-1]
    twin = {"sub": 1 - sub}
    final = picked[...].astype(BF16)

    def chip_copy(c):
        return remote(12, c, part_sums.at[c, 1 - sub], near_sums.at[c], c, twin)

    def head_copy(c, k, other):
        return remote(
            13 + c,
            k,
            chip_sums.at[c, other],
            far_sums.at[c, head],
            head,
            {"head": other},
        )

    def add_chip(c):
        chip_copy(c).wait_recv()
        chip_sums[c] = (part_sums[c, sub].astype(F32) + near_sums[c].astype(F32)).astype(BF16)
        for k, other in enumerate(heads[:-1]):
            copy = head_copy(c, k, other)
            copy.start()
            pending.append(copy)

    for c in range(chunks):
        weights = out_up[:, :, c * step : (c + 1) * step].reshape(slots * share, step)
        sums = jnp.dot(final, weights, preferred_element_type=F32).astype(BF16)
        part_sums[c, 0] = sums.reshape(n_head, 2, -1, step)[:, 0]
        part_sums[c, 1] = sums.reshape(n_head, 2, -1, step)[:, 1]
        copy = chip_copy(c)
        copy.start()
        pending.append(copy)
        if c > 0:
            add_chip(c - 1)
    add_chip(chunks - 1)
    for c in range(chunks):
        total = chip_sums[c, head].astype(F32)
        for k, other in enumerate(heads[:-1]):
            remote(
                13 + c,
                k,
                chip_sums.at[c, other],
                far_sums.at[c, other],
                other,
                {"head": other},
            ).wait_recv()
            total = total + far_sums[c, other].astype(F32)
        result[:, c * step : (c + 1) * step] = total.astype(BF16)
    for copy in pending:
        copy.wait_send()


def local_fast(
    n_row,
    n_head,
    n_sub,
    query_latent,
    kv_cache,
    row_lengths,
    head_map,
    uq_stored,
    uk_stored,
    uv_stored,
    out_stored,
):
    n = n_row * n_head
    slots, part, half = uq_stored.shape
    own, width, latent = kv_cache.shape
    rows = query_latent.shape[0]
    batch = rows * n_row
    per = slots // n
    k_part = uk_stored.shape[1]
    share = out_stored.shape[1]
    wide_out = out_stored.shape[2]
    chunks = 4
    first_slot = lax.axis_index("sub") * slots
    local_map = lax.dynamic_slice_in_dim(head_map, first_slot, slots, 0) - first_slot
    lengths = lax.dynamic_slice_in_dim(row_lengths, lax.axis_index("head") * own, own, 0)
    mask = (jnp.arange(width, dtype=jnp.int32)[None, :] < lengths[:, None]).astype(jnp.int32)
    vmem = pl.BlockSpec(memory_space=pltpu.VMEM)
    piece = pltpu.VMEM((2, n, own // 2 * per, latent), BF16)
    sums = pltpu.VMEM((chunks, n_head, batch // (n_head * n_sub), wide_out // chunks), BF16)
    return pl.pallas_call(
        functools.partial(attention_kernel, n_row, n_head, 1.0 / math.sqrt(DH)),
        out_shape=jax.ShapeDtypeStruct((batch // (n_head * n_sub), wide_out), BF16),
        in_specs=[vmem] * 3
        + [pl.BlockSpec(memory_space=pltpu.SMEM)]
        + [vmem] * 3
        + [pl.BlockSpec(memory_space=pl.ANY)],
        out_specs=vmem,
        scratch_shapes=[
            pltpu.VMEM((n_row, rows, part), BF16),
            pltpu.VMEM((n, per // 2, batch, 2 * half), BF16),
            pltpu.VMEM((n, per // 2, batch, 2 * half), BF16),
            pltpu.VMEM((n, per, half, k_part), BF16),
            pltpu.VMEM((n, per, half, k_part), BF16),
            pltpu.VMEM((batch, per, latent), F32),
            piece,
            piece,
            piece,
            piece,
            pltpu.VMEM((n_head, batch, per * share), BF16),
            pltpu.VMEM((n, batch, per * share), BF16),
            pltpu.VMEM((slots * share, slots * share), BF16),
            pltpu.VMEM((batch, slots * share), F32),
            pltpu.VMEM(out_stored.shape, BF16),
            pltpu.VMEM((chunks, n_sub) + sums.shape[1:], BF16),
            sums,
            sums,
            sums,
            pltpu.SemaphoreType.DMA((13 + chunks, n)),
            pltpu.SemaphoreType.DMA((13 + chunks, n)),
            pltpu.SemaphoreType.DMA,
        ],
        compiler_params=pltpu.CompilerParams(
            collective_id=0, has_side_effects=True, vmem_limit_bytes=56 * 1024 * 1024
        ),
    )(
        query_latent,
        kv_cache,
        mask,
        local_map,
        jnp.swapaxes(uq_stored, 1, 2),
        jnp.swapaxes(uk_stored, 1, 2),
        jnp.swapaxes(uv_stored, 1, 2),
        out_stored,
    )


def choose_local(mesh):
    n_row, n_head, n_sub = mesh.shape["row"], mesh.shape["head"], mesh.shape["sub"]

    def local(query_latent, kv_cache, row_lengths, head_map, uq, uk, uv, out_stored):
        args = (query_latent, kv_cache, row_lengths, head_map, uq, uk, uv, out_stored)
        n = n_row * n_head
        batch = query_latent.shape[0] * n_row
        fits = (
            mesh.shape["group"] == 2
            and n_sub == 2
            and n_head >= 2
            and n >= 4
            and out_stored.shape[1] % 16 == 0
            and out_stored.shape[2] % 512 == 0
            and uq.shape[0] % (8 * n) == 0
            and uq.shape[1] % 128 == 0
            and uk.shape[1] % 128 == 0
            and uq.shape[2] % 16 == 0
            and 2 * uq.shape[2] % 128 == 0
            and batch % (16 * n) == 0
            and batch % (16 * n_head * n_sub) == 0
        )
        if fits:
            return local_fast(n_row, n_head, n_sub, *args)
        return local_general(*args)

    return local


def solution(mesh):
    in_specs = (
        P(("group", "row"), None),
        P(("group", "row", "head"), None, None),
        P(("group", "row")),
        P(),
        P("sub", "head", "row"),
        P("sub", "head", "row"),
        P("sub", "head", "row"),
        P("sub", "head", "row"),
    )
    out_specs = P(("group", "head", "sub"), "row")
    local = choose_local(mesh)
    return jax.shard_map(local, mesh=mesh, in_specs=in_specs, out_specs=out_specs, check_vma=False)
```

```python
import functools
import math

import jax
import jax.numpy as jnp
from jax import lax
from jax.experimental import pallas as pl
from jax.experimental.pallas import tpu as pltpu
from jax.sharding import PartitionSpec as P

DH = 128


def form_pair(query_up, key_up, value_up, out_up):
    absorbed_q = jnp.einsum(
        "hqd,hkd->hqk", query_up, key_up, preferred_element_type=jnp.float32
    ).astype(jnp.bfloat16)
    absorbed_o = jnp.einsum(
        "hkd,hdo->hko", value_up, out_up, preferred_element_type=jnp.float32
    ).astype(jnp.bfloat16)
    return (absorbed_q, absorbed_o)


def attend(running, queries, lengths, block_rows, first_pos, score_scale):
    best, mass, accum = running
    width = block_rows.shape[1]
    scores = (
        jnp.einsum("rhk,rtk->rht", queries, block_rows, preferred_element_type=jnp.float32)
        * score_scale
    )
    positions = first_pos + jnp.arange(width, dtype=jnp.int32)
    alive = (positions[None, :] < lengths[:, None])[:, None, :]
    scores = jnp.where(alive, scores, -1e30)
    newest = jnp.maximum(best, jnp.max(scores, axis=2))
    weights = jnp.where(alive, jnp.exp(scores - newest[:, :, None]), 0.0)
    factor = jnp.exp(best - newest)
    mass = mass * factor + jnp.sum(weights, axis=2)
    accum = accum * factor[:, :, None] + jnp.einsum(
        "rht,rtk->rhk", weights, block_rows.astype(jnp.float32), precision=lax.Precision.HIGHEST
    )
    return (newest, mass, accum)


def local_general(
    query_latent, kv_cache, row_lengths, head_map, uq_stored, uk_stored, uv_stored, out_stored
):
    slots = uq_stored.shape[0]
    first_slot = lax.axis_index("sub") * slots
    local_map = lax.dynamic_slice_in_dim(head_map, first_slot, slots, 0)
    slot_order = jnp.argsort(local_map)
    query_up = jnp.take(uq_stored, slot_order, axis=0)
    key_up = jnp.take(uk_stored, slot_order, axis=0)
    value_up = jnp.take(uv_stored, slot_order, axis=0)
    query_up, key_up, value_up, out_up = (
        lax.all_to_all(query_up, "head", split_axis=0, concat_axis=1, tiled=True),
        lax.all_to_all(key_up, "head", split_axis=0, concat_axis=1, tiled=True),
        lax.all_to_all(value_up, "head", split_axis=0, concat_axis=1, tiled=True),
        lax.all_to_all(out_stored, "head", split_axis=0, concat_axis=1, tiled=True),
    )
    query_up, key_up, value_up = (
        lax.all_gather(query_up, "row", axis=2, tiled=True),
        lax.all_gather(key_up, "row", axis=2, tiled=True),
        lax.all_gather(value_up, "row", axis=2, tiled=True),
    )
    absorbed_q, absorbed_o = form_pair(query_up, key_up, value_up, out_up)
    query_lat = jnp.einsum(
        "rq,hqk->rhk", query_latent, absorbed_q, preferred_element_type=jnp.float32
    ).astype(jnp.bfloat16)
    score_scale = 1.0 / math.sqrt(DH)
    head_count = query_lat.shape[1]
    latent_width = query_lat.shape[2]
    piece = lax.all_gather(kv_cache, "head", axis=0, tiled=True)
    count = piece.shape[0]
    half = piece.shape[1] // 2
    state = (
        jnp.full((count, head_count), -1e30, jnp.float32),
        jnp.zeros((count, head_count), jnp.float32),
        jnp.zeros((count, head_count, latent_width), jnp.float32),
    )
    state = attend(state, query_lat, row_lengths, piece[:, :half], 0, score_scale)
    state = attend(state, query_lat, row_lengths, piece[:, half:], half, score_scale)
    best, mass, accum = state
    result = accum / mass[:, :, None]
    attended = result.astype(jnp.bfloat16)
    gathered = lax.all_gather(attended, "row", axis=0, tiled=True)
    summed = lax.psum_scatter(
        jnp.einsum("rhk,hko->ro", gathered, absorbed_o, preferred_element_type=jnp.float32),
        ("head", "sub"),
        scatter_dimension=0,
        tiled=True,
    )
    return summed.astype(jnp.bfloat16)


MESH = pl.DeviceIdType.MESH
F32 = jnp.float32
BF16 = jnp.bfloat16


def attention_kernel(
    n_row,
    n_head,
    scale,
    ql_ref,
    kv_hbm,
    mask_ref,
    map_ref,
    uq_hbm,
    uk_ref,
    uv_ref,
    out_hbm,
    result,
    uq_ref,
    kv_ref,
    lat,
    q_send,
    q_recv,
    uk_recv,
    uv_recv,
    wide,
    x_send,
    x_recv,
    y_send,
    y_recv,
    v_send,
    v_recv,
    pick,
    picked,
    out_up,
    part_sums,
    near_sums,
    chip_sums,
    far_sums,
    send_sem,
    recv_sem,
    load_sem,
):
    n = n_row * n_head
    group = lax.axis_index("group")
    sub = lax.axis_index("sub")
    row = lax.axis_index("row")
    head = lax.axis_index("head")
    me = row * n_head + head
    slots, half, part = uq_ref.shape
    per = slots // n
    pairs = per // 2
    rows = ql_ref.shape[0]
    batch = rows * n_row
    own = batch // n
    near = own // 2
    kept = pl.ds(group * (per // 2), per // 2)
    turns = [n_head // 2] + [d for d in range(1, n_head) if d != n_head // 2] + [0]
    shifts = [(dr, dh) for dh in turns for dr in range(n_row) if (dr, dh) != (0, 0)]
    peers = [
        lax.rem(row + dr, n_row) * n_head + lax.rem(head + dh, n_head) for dr, dh in shifts
    ]
    pending = []

    def place(peer):
        return {"row": peer // n_head, "head": lax.rem(peer, n_head)}

    def remote(phase, k, src, dst, slot, device):
        return pltpu.make_async_remote_copy(
            src_ref=src,
            dst_ref=dst,
            send_sem=send_sem.at[phase, k],
            recv_sem=recv_sem.at[phase, slot],
            device_id=device,
            device_id_type=MESH,
        )

    def send(phase, k, src, dst, peer):
        copy = remote(phase, k, src, dst, me, place(peer))
        copy.start()
        pending.append(copy)

    def arrived(phase, k, dst, peer):
        remote(phase, k, dst, dst, peer, place(peer)).wait_recv()

    def send_weights(phase, src, dst):
        for k, peer in enumerate(peers):
            first = peer * per + group * (per // 2)
            send(phase, k, src.at[pl.ds(first, per // 2)], dst.at[me, kept], peer)

    def pass_weights(phase, dst):
        for k, peer in enumerate(peers):
            arrived(phase, k, dst.at[peer, kept], peer)
            block = dst.at[peer, kept]
            copy = remote(phase + 1, k, block, block, peer, {"group": 1 - group})
            copy.start()
            pending.append(copy)

    def await_weights(phase, dst):
        other = pl.ds((1 - group) * (per // 2), per // 2)
        for k, peer in enumerate(peers):
            block = dst.at[peer, other]
            remote(phase + 1, k, block, block, peer, {"group": 1 - group}).wait_recv()

    uq_load = pltpu.make_async_copy(uq_hbm, uq_ref, load_sem.at[1])
    kv_load = pltpu.make_async_copy(kv_hbm, kv_ref, load_sem.at[2])
    mine = pl.ds(me * per, per)
    uk_load = pltpu.make_async_copy(uk_ref.at[mine], uk_recv.at[me], load_sem.at[3])
    uv_load = pltpu.make_async_copy(uv_ref.at[mine], uv_recv.at[me], load_sem.at[4])
    uq_load.start()
    barrier = pltpu.get_barrier_semaphore()
    for peer in peers:
        pl.semaphore_signal(barrier, inc=1, device_id=place(peer), device_id_type=MESH)
    pl.semaphore_signal(barrier, inc=1, device_id={"group": 1 - group}, device_id_type=MESH)
    pl.semaphore_signal(barrier, inc=1, device_id={"sub": 1 - sub}, device_id_type=MESH)
    pl.semaphore_wait(barrier, n + 1)

    columns = pl.ds(pl.multiple_of(head * part, 128), part)
    others = [lax.rem(row + k, n_row) for k in range(1, n_row)]
    for k, other in enumerate(others):
        send(0, k, ql_ref.at[:, columns], lat.at[row], other * n_head + head)
    send_weights(2, uk_ref, uk_recv)
    load = pltpu.make_async_copy(out_hbm, out_up, load_sem.at[0])
    lat[row] = ql_ref[:, columns]
    for k, other in enumerate(others):
        arrived(0, k, lat.at[other], other * n_head + head)
    latent = lat[...].reshape(batch, part)
    uq_load.wait()

    for k, peer in enumerate(peers + [me]):
        for at in range(pairs):
            two = uq_ref[pl.ds(peer * per + 2 * at, 2)].reshape(2 * half, part)
            both = lax.dot_general(
                latent, two, (((1,), (1,)), ((), ())), preferred_element_type=F32
            ).astype(BF16)
            if k < n - 1:
                q_send[peer, at] = both
            else:
                q_recv[me, at] = both
        if k < n - 1:
            send(1, k, q_send.at[peer], q_recv.at[me], peer)
    send_weights(8, uv_ref, uv_recv)
    uk_load.start()
    uv_load.start()
    kv_load.start()
    load.start()
    pass_weights(2, uk_recv)

    share = out_hbm.shape[1]
    spots = lax.broadcasted_iota(jnp.int32, (share, slots * share), 1)
    spots = spots - lax.broadcasted_iota(jnp.int32, (share, slots * share), 0)

    def mark(slot, carry):
        lanes = spots == map_ref[slot] * share
        first = pl.multiple_of(slot * share, share)
        pick[pl.ds(first, share), :] = jnp.where(lanes, 1.0, 0.0).astype(BF16)
        return carry

    lax.fori_loop(0, slots, mark, 0)

    for k, peer in enumerate(peers):
        arrived(1, k, q_recv.at[peer], peer)
    queries = []
    for at in range(pairs):
        sums = []
        for r in range(n_row):
            total = q_recv[r * n_head, at].astype(F32)
            for h in range(1, n_head):
                total = total + q_recv[r * n_head + h, at].astype(F32)
            sums.append(total.astype(BF16))
        for which in range(2):
            queries.append(
                jnp.concatenate([s[:, which * half : (which + 1) * half] for s in sums], axis=1)
            )
    await_weights(2, uk_recv)
    uk_load.wait()
    uv_load.wait()
    kv_load.wait()

    def joined(ref, slot):
        return jnp.concatenate(
            [
                jnp.concatenate([ref[r * n_head + h, slot] for h in range(n_head)], axis=1)
                for r in range(n_row)
            ],
            axis=0,
        )

    for slot in range(per):
        wide[:, slot, :] = jnp.dot(
            queries[slot], joined(uk_recv, slot), preferred_element_type=F32
        )
    for part_at in range(2):
        for k, peer in enumerate(peers + [me]):
            block = wide[pl.ds(peer * own + part_at * near, near)]
            block = block.reshape(near * per, -1).astype(BF16)
            if k < n - 1:
                x_send[part_at, peer] = block
                send(
                    4 + part_at, k, x_send.at[part_at, peer], x_recv.at[part_at, me], peer
                )
            else:
                x_recv[part_at, me] = block
    pass_weights(8, uv_recv)

    for part_at in range(2):
        for k, peer in enumerate(peers):
            arrived(4 + part_at, k, x_recv.at[part_at, peer], peer)
        wanted = x_recv[part_at].astype(F32)
        scores = []
        for b in range(near):
            query = wanted[:, b * per : (b + 1) * per].reshape(slots, -1).astype(BF16)
            score = (
                lax.dot_general(
                    query,
                    kv_ref[part_at * near + b],
                    (((1,), (1,)), ((), ())),
                    preferred_element_type=F32,
                )
                * scale
            )
            at = part_at * near + b
            scores.append(jnp.where(mask_ref[at : at + 1, :] > 0, score, -1e30))
        stacked = jnp.concatenate(scores, axis=0)
        top = jnp.max(stacked, axis=1, keepdims=True)
        weights = jnp.exp(stacked - top)
        mass = jnp.sum(weights, axis=1, keepdims=True)
        weights = (weights / mass).astype(BF16)
        for b in range(near):
            mixed = jnp.dot(
                weights[b * slots : (b + 1) * slots],
                kv_ref[part_at * near + b],
                preferred_element_type=F32,
            )
            for p in range(n):
                wide[p * own + part_at * near + b] = mixed[p * per : (p + 1) * per]
        for k, peer in enumerate(peers + [me]):
            block = wide[pl.ds(peer * own + part_at * near, near)]
            block = block.reshape(near * per, -1).astype(BF16)
            if k < n - 1:
                y_send[part_at, peer] = block
                send(
                    6 + part_at, k, y_send.at[part_at, peer], y_recv.at[part_at, me], peer
                )
            else:
                y_recv[part_at, me] = block
    await_weights(8, uv_recv)
    for part_at in range(2):
        for k, peer in enumerate(peers):
            arrived(6 + part_at, k, y_recv.at[part_at, peer], peer)
        for p in range(n):
            first = p * own + part_at * near
            wide[first : first + near] = (
                y_recv[part_at, p].astype(F32).reshape(near, per, wide.shape[2])
            )
    values = []
    for slot in range(per):
        values.append(
            lax.dot_general(
                wide[:, slot, :].astype(BF16),
                joined(uv_recv, slot),
                (((1,), (1,)), ((), ())),
                preferred_element_type=F32,
            ).astype(BF16)
        )
    for h in range(n_head):
        v_send[h] = jnp.concatenate([v[:, h * share : (h + 1) * share] for v in values], axis=1)
    heads = [lax.rem(head + d, n_head) for d in turns]
    v_recv[me] = v_send[head]
    for k, other in enumerate(heads[:-1]):
        send(10, k, v_send.at[other], v_recv.at[me], row * n_head + other)

    def forward(k, peer):
        for i, other in enumerate(others):
            copy = remote(
                11,
                k * (n_row - 1) + i,
                v_recv.at[peer],
                v_recv.at[peer],
                peer,
                place(other * n_head + head),
            )
            copy.start()
            pending.append(copy)

    deep = per * share

    def spread(peer, fresh):
        rows_of = pl.ds(pl.multiple_of(peer * deep, deep), deep)
        term = jnp.dot(v_recv[peer], pick[rows_of, :], preferred_element_type=F32)
        picked[...] = term if fresh else picked[...] + term

    forward(n_head - 1, me)
    spread(me, True)
    for k, other in enumerate(heads[:-1]):
        peer = row * n_head + other
        arrived(10, k, v_recv.at[peer], peer)
        forward(k, peer)
        spread(peer, False)
    for i, away in enumerate(others):
        for k, other in enumerate([heads[-1]] + heads[:-1]):
            peer = away * n_head + other
            remote(
                11, 0, v_recv.at[peer], v_recv.at[peer], peer, place(away * n_head + head)
            ).wait_recv()
            spread(peer, False)

    load.wait()
    chunks, step = part_sums.shape[0], part_sums.shape[-1]
    twin = {"sub": 1 - sub}
    final = picked[...].astype(BF16)

    def chip_copy(c):
        return remote(12, c, part_sums.at[c, 1 - sub], near_sums.at[c], c, twin)

    def head_copy(c, k, other):
        return remote(
            13 + c,
            k,
            chip_sums.at[c, other],
            far_sums.at[c, head],
            head,
            {"head": other},
        )

    def add_chip(c):
        chip_copy(c).wait_recv()
        chip_sums[c] = (part_sums[c, sub].astype(F32) + near_sums[c].astype(F32)).astype(BF16)
        for k, other in enumerate(heads[:-1]):
            copy = head_copy(c, k, other)
            copy.start()
            pending.append(copy)

    for c in range(chunks):
        weights = out_up[:, :, c * step : (c + 1) * step].reshape(slots * share, step)
        sums = jnp.dot(final, weights, preferred_element_type=F32).astype(BF16)
        part_sums[c, 0] = sums.reshape(n_head, 2, -1, step)[:, 0]
        part_sums[c, 1] = sums.reshape(n_head, 2, -1, step)[:, 1]
        copy = chip_copy(c)
        copy.start()
        pending.append(copy)
        if c > 0:
            add_chip(c - 1)
    add_chip(chunks - 1)
    for c in range(chunks):
        total = chip_sums[c, head].astype(F32)
        for k, other in enumerate(heads[:-1]):
            remote(
                13 + c,
                k,
                chip_sums.at[c, other],
                far_sums.at[c, other],
                other,
                {"head": other},
            ).wait_recv()
            total = total + far_sums[c, other].astype(F32)
        result[:, c * step : (c + 1) * step] = total.astype(BF16)
    for copy in pending:
        copy.wait_send()


def local_fast(
    n_row,
    n_head,
    n_sub,
    query_latent,
    kv_cache,
    row_lengths,
    head_map,
    uq_stored,
    uk_stored,
    uv_stored,
    out_stored,
):
    n = n_row * n_head
    slots, part, half = uq_stored.shape
    own, width, latent = kv_cache.shape
    rows = query_latent.shape[0]
    batch = rows * n_row
    per = slots // n
    k_part = uk_stored.shape[1]
    share = out_stored.shape[1]
    wide_out = out_stored.shape[2]
    chunks = 4
    first_slot = lax.axis_index("sub") * slots
    local_map = lax.dynamic_slice_in_dim(head_map, first_slot, slots, 0) - first_slot
    lengths = lax.dynamic_slice_in_dim(row_lengths, lax.axis_index("head") * own, own, 0)
    mask = (jnp.arange(width, dtype=jnp.int32)[None, :] < lengths[:, None]).astype(jnp.int32)
    vmem = pl.BlockSpec(memory_space=pltpu.VMEM)
    piece = pltpu.VMEM((2, n, own // 2 * per, latent), BF16)
    sums = pltpu.VMEM((chunks, n_head, batch // (n_head * n_sub), wide_out // chunks), BF16)
    return pl.pallas_call(
        functools.partial(attention_kernel, n_row, n_head, 1.0 / math.sqrt(DH)),
        out_shape=jax.ShapeDtypeStruct((batch // (n_head * n_sub), wide_out), BF16),
        in_specs=[
            vmem,
            pl.BlockSpec(memory_space=pl.ANY),
            vmem,
            pl.BlockSpec(memory_space=pltpu.SMEM),
        ]
        + [pl.BlockSpec(memory_space=pl.ANY)] * 4,
        out_specs=vmem,
        scratch_shapes=[
            pltpu.VMEM((slots, half, part), BF16),
            pltpu.VMEM(kv_cache.shape, BF16),
            pltpu.VMEM((n_row, rows, part), BF16),
            pltpu.VMEM((n, per // 2, batch, 2 * half), BF16),
            pltpu.VMEM((n, per // 2, batch, 2 * half), BF16),
            pltpu.VMEM((n, per, half, k_part), BF16),
            pltpu.VMEM((n, per, half, k_part), BF16),
            pltpu.VMEM((batch, per, latent), F32),
            piece,
            piece,
            piece,
            piece,
            pltpu.VMEM((n_head, batch, per * share), BF16),
            pltpu.VMEM((n, batch, per * share), BF16),
            pltpu.VMEM((slots * share, slots * share), BF16),
            pltpu.VMEM((batch, slots * share), F32),
            pltpu.VMEM(out_stored.shape, BF16),
            pltpu.VMEM((chunks, n_sub) + sums.shape[1:], BF16),
            sums,
            sums,
            sums,
            pltpu.SemaphoreType.DMA((13 + chunks, n)),
            pltpu.SemaphoreType.DMA((13 + chunks, n)),
            pltpu.SemaphoreType.DMA((5,)),
        ],
        compiler_params=pltpu.CompilerParams(
            collective_id=0, has_side_effects=True, vmem_limit_bytes=60 * 1024 * 1024
        ),
    )(
        query_latent,
        kv_cache,
        mask,
        local_map,
        jnp.swapaxes(uq_stored, 1, 2),
        jnp.swapaxes(uk_stored, 1, 2),
        jnp.swapaxes(uv_stored, 1, 2),
        out_stored,
    )


def choose_local(mesh):
    n_row, n_head, n_sub = mesh.shape["row"], mesh.shape["head"], mesh.shape["sub"]

    def local(query_latent, kv_cache, row_lengths, head_map, uq, uk, uv, out_stored):
        args = (query_latent, kv_cache, row_lengths, head_map, uq, uk, uv, out_stored)
        n = n_row * n_head
        batch = query_latent.shape[0] * n_row
        fits = (
            mesh.shape["group"] == 2
            and n_sub == 2
            and n_head >= 2
            and n >= 4
            and out_stored.shape[1] % 16 == 0
            and out_stored.shape[2] % 512 == 0
            and uq.shape[0] % (8 * n) == 0
            and uq.shape[1] % 128 == 0
            and uk.shape[1] % 128 == 0
            and uq.shape[2] % 16 == 0
            and 2 * uq.shape[2] % 128 == 0
            and batch % (16 * n) == 0
            and batch % (16 * n_head * n_sub) == 0
        )
        if fits:
            return local_fast(n_row, n_head, n_sub, *args)
        return local_general(*args)

    return local


def solution(mesh):
    in_specs = (
        P(("group", "row"), None),
        P(("group", "row", "head"), None, None),
        P(("group", "row")),
        P(),
        P("sub", "head", "row"),
        P("sub", "head", "row"),
        P("sub", "head", "row"),
        P("sub", "head", "row"),
    )
    out_specs = P(("group", "head", "sub"), "row")
    local = choose_local(mesh)
    return jax.shard_map(local, mesh=mesh, in_specs=in_specs, out_specs=out_specs, check_vma=False)
```
